256 devices in a mesh: dp: 8 (over x, core), seq: 32 (over z, y).
Axes of the slice: x: 4, y: 4, z: 8, core: 2. Of those that a mesh axis runs over, the one named last changes fastest.
Arguments:
- queries: bfloat16 [65536, 16, 128], P(('dp', 'seq')), parts along dimension 0, may hold values from -6 to 6
- keys: bfloat16 [65536, 16, 128], P(('dp', 'seq')), parts along dimension 0, may hold values from -6 to 6
- values: bfloat16 [65536, 16, 128], P(('dp', 'seq')), parts along dimension 0, may hold values from -6 to 6
- cotangent: bfloat16 [65536, 16, 128], P(('dp', 'seq')), parts along dimension 0, may hold values from -6 to 6
- doc_lengths: int32 [192], P('dp'), parts along dimension 0, may hold values from 1 to 2048, 8192 in all
Outputs:
- attended: bfloat16 [65536, 16, 128], P(('dp', 'seq')), parts along dimension 0
- grad_queries: bfloat16 [65536, 16, 128], P(('dp', 'seq')), parts along dimension 0
- grad_keys: bfloat16 [65536, 16, 128], P(('dp', 'seq')), parts along dimension 0
- grad_values: bfloat16 [65536, 16, 128], P(('dp', 'seq')), parts along dimension 0
The draws below stay inside these ranges and needn't reach their ends.
There are 8 independent parts, one for each index of `dp`. The reference program is written for one: setup_inputs(seed, part) draws one part's arguments, and reference() takes and returns one part's arrays. A program takes and returns all parts, laid end to end along the dimension named above; each array names one. Nothing has to cross between parts.
Inputs may be any that keep to these rules, and one draw needn't show every extreme that they name: `doc_lengths`: the lengths sum to 8192, and the longest document has exactly 2048 positions.
All inputs are finite; a program needn't handle non-finite values.
Results may differ from the reference program's by a relative error of at most 0.005.
Values sent between devices are 32-bit elements; how exact they have to be, the bound alone decides.
No kernel may reach another device: no remote copies, remote signals or barrier semaphores. Data moves between devices by JAX's collectives and lax.ppermute only.
A program may use at most 64 MiB of HBM per device.

```python
import math
import jax
import jax.numpy as jnp
import numpy as np
from jax import lax

HEADS = 16
DK = 128
DV = 128
BLOCK = 256
DOCS = 24
TOKENS = 8192
MOST = 2048


def shard_levels(own_key, extent, cuts, least, largest):
    level = 1.0
    for axis_at, blocks in cuts:
        draws = jax.random.uniform(jax.random.fold_in(jax.random.fold_in(own_key, 6), axis_at), (blocks,), jnp.float32, least / len(cuts), largest / len(cuts))
        level = level * jnp.repeat(jnp.exp(draws), extent[axis_at] // blocks).reshape((-1,) + (1,) * (len(extent) - 1 - axis_at))
    return level


def profile(count, total, most, skew):
    weights = [(1 << 20) // math.isqrt(grade ** skew) + 1 for grade in range(2, count + 1)]
    spare, given = total - most - (count - 1), [1] * (count - 1)
    while spare > 0:
        candidates = [i for i in range(count - 1) if given[i] < most]
        whole, remaining = sum([weights[i] for i in candidates]), spare
        for i in candidates:
            more = min(most - given[i], max(1, remaining * weights[i] // whole), spare)
            given[i] = given[i] + more
            spare = spare - more
    return np.array([most] + given)


def uneven(stream_key, amount, total, bound, skew):
    if amount == 2:
        one = jax.random.randint(stream_key, (), max(1, total - bound), min(bound, total - 1) + 1)
        return jnp.stack([one, total - one])
    lengths = jnp.asarray(profile(amount, total, bound, skew), jnp.int32)
    pairs = (amount - 1) // 2
    donor, sink = lengths[1:1 + 2 * pairs:2], lengths[2:2 + 2 * pairs:2]
    margin = jnp.minimum(donor - 1, bound - sink)
    moved = jax.random.randint(jax.random.fold_in(stream_key, 1), (pairs,), 0, 1 << 20) % (margin + 1)
    lengths = lengths.at[1:1 + 2 * pairs:2].set(donor - moved).at[2:2 + 2 * pairs:2].set(sink + moved)
    return lengths[jax.random.permutation(jax.random.fold_in(stream_key, 2), amount)]


def bell_draw(rng, shape, scale, reach, shards=(), kind=jnp.bfloat16):
    array = scale * jax.random.normal(rng, shape, jnp.float32)
    if shards:
        array = array * shard_levels(rng, shape, shards, -0.22, 0.18)
    return jnp.clip(array, -reach, reach).astype(kind)


def setup_inputs(seed: int = 0, part: int = 0) -> dict:
    key_of = jax.random.split(jax.random.key(seed), 6)
    part_splits = jax.random.split(jax.random.fold_in(key_of[5], part), 6)
    return {
        "queries": bell_draw(part_splits[0], (TOKENS, HEADS, DK), 1.0, 6.0, ((0, 32),)),
        "keys": bell_draw(part_splits[1], (TOKENS, HEADS, DK), 1.0, 6.0, ((0, 32),)),
        "values": bell_draw(part_splits[2], (TOKENS, HEADS, DV), 1.0, 6.0, ((0, 32),)),
        "cotangent": bell_draw(part_splits[3], (TOKENS, HEADS, DV), 1.0, 6.0, ((0, 32),)),
        "doc_lengths": uneven(part_splits[4], DOCS, TOKENS, MOST, 2).astype(jnp.int32),
    }


def doc_index(doc_lengths):
    doc_ends = jnp.cumsum(doc_lengths).astype(jnp.int32)
    positions = jnp.arange(TOKENS, dtype=jnp.int32)
    return jnp.sum((positions[:, None] >= doc_ends[None, :]).astype(jnp.int32), axis=1).astype(jnp.int32)


def block_outputs(pieces):
    query_blk, key_blk, value_blk, cot_blk, block_ids, state_in, return_in = pieces
    factor = (DK * BLOCK) ** -0.5
    places = jnp.arange(BLOCK, dtype=jnp.int32)
    visible = (block_ids[:, None] == block_ids[None, :]) & (places[:, None] >= places[None, :])
    query_f = query_blk.astype(jnp.float32)
    key_f = key_blk.astype(jnp.float32)
    value_f = value_blk.astype(jnp.float32)
    cot_f = cot_blk.astype(jnp.float32)
    scores = jnp.einsum("thd,shd->hts", query_f, key_f)
    weights = jnp.where(visible[None], factor * scores, 0.0).astype(jnp.bfloat16).astype(jnp.float32)
    grad_scores = jnp.einsum("the,she->hts", cot_f, value_f)
    grad_weights = jnp.where(visible[None], factor * grad_scores, 0.0).astype(jnp.bfloat16).astype(jnp.float32)
    head_in = (block_ids == block_ids[0]).astype(jnp.float32)[:, None, None]
    tail_in = (block_ids == block_ids[-1]).astype(jnp.float32)[:, None, None]
    state_f = state_in.astype(jnp.float32)
    return_f = return_in.astype(jnp.float32)
    attended = jnp.einsum("hts,she->the", weights, value_f) + factor * head_in * jnp.einsum("thd,hde->the", query_f, state_f)
    grad_q = jnp.einsum("hts,shd->thd", grad_weights, key_f) + factor * head_in * jnp.einsum("the,hde->thd", cot_f, state_f)
    grad_k = jnp.einsum("hts,thd->shd", grad_weights, query_f) + factor * tail_in * jnp.einsum("she,hde->shd", value_f, return_f)
    grad_v = jnp.einsum("hts,the->she", weights, cot_f) + factor * tail_in * jnp.einsum("shd,hde->she", key_f, return_f)
    return (attended.astype(jnp.bfloat16), grad_q.astype(jnp.bfloat16), grad_k.astype(jnp.bfloat16), grad_v.astype(jnp.bfloat16))


def reference(queries, keys, values, cotangent, doc_lengths):
    ident = doc_index(doc_lengths)
    count = TOKENS // BLOCK
    query_b = queries.reshape(count, BLOCK, HEADS, DK)
    key_b = keys.reshape(count, BLOCK, HEADS, DK)
    value_b = values.reshape(count, BLOCK, HEADS, DV)
    cot_b = cotangent.reshape(count, BLOCK, HEADS, DV)
    id_b = ident.reshape(count, BLOCK)
    next_first = jnp.concatenate([id_b[1:, 0], jnp.full((1,), -1, jnp.int32)])
    prev_last = jnp.concatenate([jnp.full((1,), -1, jnp.int32), id_b[:-1, -1]])
    zero_state = jnp.zeros((HEADS, DK, DV), jnp.float32)

    def forward_step(running, pieces):
        key_blk, value_blk, block_ids, target = pieces
        masked = jnp.where((block_ids == target)[:, None, None], key_blk.astype(jnp.float32), 0.0)
        addend = jnp.einsum("shd,she->hde", masked, value_blk.astype(jnp.float32))
        keep_on = (block_ids[0] == target).astype(jnp.float32)
        return addend + keep_on * running, running

    def backward_step(running, pieces):
        query_blk, cot_blk, block_ids, target = pieces
        masked = jnp.where((block_ids == target)[:, None, None], query_blk.astype(jnp.float32), 0.0)
        addend = jnp.einsum("thd,the->hde", masked, cot_blk.astype(jnp.float32))
        keep_on = (block_ids[-1] == target).astype(jnp.float32)
        return addend + keep_on * running, running

    _, state_sum = lax.scan(forward_step, zero_state, (key_b, value_b, id_b, next_first))
    _, return_sum = lax.scan(backward_step, zero_state, (query_b, cot_b, id_b, prev_last), reverse=True)
    carried = state_sum.astype(jnp.bfloat16)
    returned = return_sum.astype(jnp.bfloat16)
    attended, grad_q, grad_k, grad_v = lax.map(block_outputs, (query_b, key_b, value_b, cot_b, id_b, carried, returned))
    return (attended.reshape(TOKENS, HEADS, DV), grad_q.reshape(TOKENS, HEADS, DK), grad_k.reshape(TOKENS, HEADS, DK), grad_v.reshape(TOKENS, HEADS, DV))
```

```python
import functools

import jax
import jax.numpy as jnp
from jax import lax
from jax.experimental import pallas as pl
from jax.experimental.pallas import tpu as pltpu
from jax.sharding import PartitionSpec as P

BLOCK = 256
RING = 4
PARTS = 1
F32 = jnp.float32
BF16 = jnp.bfloat16
IN_VMEM = pl.BlockSpec(memory_space=pltpu.VMEM)
IN_SMEM = pl.BlockSpec(memory_space=pltpu.SMEM)
VMEM_BYTES = 28 * 1024 * 1024
FORWARD, BACKWARD, OPEN_F, OPEN_B, FAR = 0, 20, 40, 44, 48
TABLE = 50


def along_y(block, distance, groups):
    route = [
        (z * RING + y, z * RING + (y + distance) % RING) for z in range(groups) for y in range(RING)
    ]
    return lax.ppermute(block, "seq", route)


def along_z(block, distance, groups):
    route = [
        (z * RING + y, (z + distance) * RING + y)
        for z in range(groups)
        for y in range(RING)
        if 0 <= z + distance < groups
    ]
    return lax.ppermute(block, "seq", route)


def dot(left, right, left_dim, right_dim):
    return lax.dot_general(
        left, right, (((left_dim,), (right_dim,)), ((), ())), preferred_element_type=F32
    )


def ends_of(lens):
    ends, total = [], jnp.int32(0)
    for d in range(lens.shape[0]):
        total = total + lens[d]
        ends.append(total)
    return ends


def start_at(ends, position):
    start = jnp.int32(0)
    for end in ends:
        start = jnp.where(end <= position, end, start)
    return start


def end_at(ends, position):
    found = jnp.int32(1 << 20)
    for end in reversed(ends):
        found = jnp.where(end > position, end, found)
    return found


def rows_where(shape, dim, low, high):
    places = lax.broadcasted_iota(jnp.int32, shape, dim)
    return ((places >= low) & (places < high)).astype(F32)


def addend_kernel(heads, rank, lens, q, k, v, c, *outs_and_scratch):
    outs, (qs, ks, vs, cs) = outs_and_scratch[:-4], outs_and_scratch[-4:]
    rows, width = q.shape[0], q.shape[2]
    first = rank[0] * rows
    ring = lax.rem(rank[0], RING)
    ends = ends_of(lens)
    tail_from = start_at(ends, first + rows) - first
    head_to = jnp.where(first > 0, end_at(ends, first - 1) - first, 0)
    tail = rows_where((rows, width), 0, tail_from, rows).astype(BF16)
    head = rows_where((rows, width), 0, 0, head_to).astype(BF16)
    for ref, scratch in ((k, ks), (v, vs), (q, qs), (c, cs)):
        scratch[...] = jnp.swapaxes(ref[...], 0, 1)
    own = heads // (RING * PARTS)
    for part in range(PARTS):
        for r in range(RING):
            owner = lax.rem(ring + r, RING)
            out = outs[part * RING + r]
            for j in range(own):
                h = part * (heads // PARTS) + owner * own + j
                out[0, j] = dot(ks[h] * tail, vs[h], 0, 0)
                out[1, j] = dot(qs[h] * head, cs[h], 0, 0)


def inner_kernel(heads, factor, rank, lens, q, k, v, c, qs, ks, vs, cs, att, gq, gk, gv, table):
    rows = q.shape[0]
    first = rank[0] * rows
    ends = ends_of(lens)

    def same(a, b):
        cut = jnp.int32(0)
        for end in ends:
            cut = cut | ((end > a) & (end <= b)).astype(jnp.int32)
        return 1 - cut

    start = lax.div(rank[0], RING) * RING * rows
    step_f = [same(start + j * rows, start + (j + 1) * rows) for j in range(RING)]
    step_b = [same(start + j * rows - 1, start + (j + 1) * rows - 1) for j in range(RING)]
    for t in range(RING + 1):
        for s in range(RING):
            weight = jnp.int32(1 if s < t else 0)
            for j in range(s + 1, t):
                weight = weight * step_f[j]
            table[FORWARD + t * RING + s] = weight.astype(F32)
    for t in range(RING + 1):
        for s in range(RING):
            weight = jnp.int32(1 if s > t - 1 else 0)
            for j in range(t, s):
                weight = weight * step_b[j]
            table[BACKWARD + t * RING + s] = weight.astype(F32)
    weight = jnp.int32(1)
    for t in range(RING):
        table[OPEN_F + t] = weight.astype(F32)
        weight = weight * step_f[t]
    weight = jnp.int32(1)
    for t in reversed(range(RING)):
        table[OPEN_B + t] = weight.astype(F32)
        weight = weight * step_b[t]
    table[FAR] = same(start - RING * rows, start).astype(F32)
    table[FAR + 1] = same(start + RING * rows - 1, start + 2 * RING * rows - 1).astype(F32)

    for ref, out in ((q, qs), (k, ks), (v, vs), (c, cs)):
        out[...] = jnp.swapaxes(ref[...], 0, 1)
    t_at = first + lax.broadcasted_iota(jnp.int32, (rows, rows), 0)
    s_at = first + lax.broadcasted_iota(jnp.int32, (rows, rows), 1)
    end_of = jnp.full((1, rows), 1 << 20, jnp.int32)
    lane = first + lax.broadcasted_iota(jnp.int32, (1, rows), 1)
    for end in reversed(ends):
        end_of = jnp.where(lane < end, end, end_of)
    visible = jnp.where((t_at >= s_at) & (t_at < end_of), factor, 0.0)

    def one(h, carry):
        qh, kh, vh, ch = qs[h], ks[h], vs[h], cs[h]
        weights = (visible * dot(qh, kh, 1, 1)).astype(BF16)
        grads = (visible * dot(ch, vh, 1, 1)).astype(BF16)
        att[h] = dot(weights, vh, 1, 0).astype(BF16)
        gq[h] = dot(grads, kh, 1, 0).astype(BF16)
        gk[h] = dot(grads, qh, 0, 0).astype(BF16)
        gv[h] = dot(weights, ch, 0, 0).astype(BF16)
        return carry

    lax.fori_loop(0, heads, one, 0, unroll=2)


def total_kernel(rank, table, *refs):
    held, (total_f, total_b) = refs[:RING], refs[RING:]
    ring = lax.rem(rank[0], RING)
    for direction, out, row in ((0, total_f, FORWARD + RING * RING), (1, total_b, BACKWARD)):
        total = None
        for r in range(RING):
            source = lax.rem(ring + RING - r, RING)
            term = table[row + source] * held[r][direction]
            total = term if total is None else total + term
        out[...] = total


def carry_kernel(rank, table, *refs):
    held, (near_f, far_f, near_b, far_b), outs = refs[:RING], refs[RING : RING + 4], refs[RING + 4 :]
    ring = lax.rem(rank[0], RING)
    into = (near_f[...] + table[FAR] * far_f[...], near_b[...] + table[FAR + 1] * far_b[...])
    for r in range(RING):
        target = lax.rem(ring + r, RING)
        for direction in range(2):
            row = FORWARD + target * RING if direction == 0 else BACKWARD + (target + 1) * RING
            total = table[(OPEN_F if direction == 0 else OPEN_B) + target] * into[direction]
            for s in range(RING):
                source = lax.rem(ring + RING - s, RING)
                total = total + table[row + source] * held[s][direction]
            outs[r][direction] = total


def outer_kernel(heads, factor, rank, lens, qs, ks, vs, cs, att, gq, gk, gv, *refs):
    states, outs, scratch = refs[: RING * PARTS], refs[RING * PARTS : RING * PARTS + 4], refs[-4:]
    rows, width = qs.shape[1], qs.shape[2]
    first = rank[0] * rows
    ring = lax.rem(rank[0], RING)
    ends = ends_of(lens)
    head = factor * rows_where((rows, width), 0, 0, end_at(ends, first) - first)
    tail = factor * rows_where((rows, width), 0, start_at(ends, first + rows - 1) - first, rows)
    own = heads // (RING * PARTS)
    for part in range(PARTS):
        for r in range(RING):
            owner = lax.rem(ring + RING - r, RING)
            both = states[part * RING + r]
            for j in range(own):
                h = part * (heads // PARTS) + owner * own + j
                state, back = both[0, j].astype(BF16), both[1, j].astype(BF16)
                scratch[0][h] = (att[h].astype(F32) + head * dot(qs[h], state, 1, 0)).astype(BF16)
                scratch[1][h] = (gq[h].astype(F32) + head * dot(cs[h], state, 1, 1)).astype(BF16)
                scratch[2][h] = (gk[h].astype(F32) + tail * dot(vs[h], back, 1, 1)).astype(BF16)
                scratch[3][h] = (gv[h].astype(F32) + tail * dot(ks[h], back, 1, 0)).astype(BF16)
    for out, ref in zip(outs, scratch):
        out[...] = jnp.swapaxes(ref[...], 0, 1)


def local(queries, keys, values, cotangent, doc_lengths):
    rows, heads, width = queries.shape
    groups = lax.axis_size("seq") // RING
    rank = lax.axis_index("seq").astype(jnp.int32).reshape(1)
    factor = (width * BLOCK) ** (-0.5)
    own = heads // (RING * PARTS)
    shape = jax.ShapeDtypeStruct
    chunk = shape((2, own, width, width), F32)
    single = shape((own, width, width), F32)
    major = shape((heads, rows, width), BF16)
    params = pltpu.CompilerParams(vmem_limit_bytes=VMEM_BYTES)
    given = (queries, keys, values, cotangent)

    addends = pl.pallas_call(
        functools.partial(addend_kernel, heads),
        out_shape=[chunk] * (RING * PARTS),
        in_specs=[IN_SMEM] * 2 + [IN_VMEM] * 4,
        out_specs=[IN_VMEM] * (RING * PARTS),
        scratch_shapes=[pltpu.VMEM((heads, rows, width), BF16)] * 4,
        compiler_params=params,
        name="addends",
    )(rank, doc_lengths, *given)
    held = [
        [along_y(addends[p * RING + r], r, groups) if r else addends[p * RING] for r in range(RING)]
        for p in range(PARTS)
    ]
    inner = pl.pallas_call(
        functools.partial(inner_kernel, heads, factor),
        out_shape=[major] * 8 + [shape((TABLE,), F32)],
        in_specs=[IN_SMEM] * 2 + [IN_VMEM] * 4,
        out_specs=[IN_VMEM] * 8 + [IN_SMEM],
        compiler_params=params,
        cost_estimate=pl.CostEstimate(flops=2 * 10**9, bytes_accessed=12 << 20, transcendentals=0),
        name="inner",
    )(rank, doc_lengths, *given)
    table = inner[8]
    states = []
    for part in held:
        total_f, total_b = pl.pallas_call(
            total_kernel,
            out_shape=[single] * 2,
            in_specs=[IN_SMEM] * 2 + [IN_VMEM] * RING,
            out_specs=[IN_VMEM] * 2,
            compiler_params=params,
            name="totals",
        )(rank, table, *part)
        around = (
            along_z(total_f, 1, groups),
            along_z(total_f, 2, groups),
            along_z(total_b, -1, groups),
            along_z(total_b, -2, groups),
        )
        carries = pl.pallas_call(
            carry_kernel,
            out_shape=[chunk] * RING,
            in_specs=[IN_SMEM] * 2 + [IN_VMEM] * (RING + 4),
            out_specs=[IN_VMEM] * RING,
            compiler_params=params,
            name="carries",
        )(rank, table, *part, *around)
        states += [along_y(carries[r], r, groups) if r else carries[0] for r in range(RING)]
    return tuple(
        pl.pallas_call(
            functools.partial(outer_kernel, heads, factor),
            out_shape=[shape((rows, heads, width), BF16)] * 4,
            in_specs=[IN_SMEM] * 2 + [IN_VMEM] * (8 + RING * PARTS),
            out_specs=[IN_VMEM] * 4,
            scratch_shapes=[pltpu.VMEM((heads, rows, width), BF16)] * 4,
            compiler_params=params,
            name="outer",
        )(rank, doc_lengths, *inner[:8], *states)
    )


def solution(mesh):
    rows = P(("dp", "seq"), None, None)
    return jax.shard_map(
        local, mesh=mesh, in_specs=(rows, rows, rows, rows, P("dp")), out_specs=(rows,) * 4, check_vma=False
    )
```

```python
import functools

import jax
import jax.numpy as jnp
from jax import lax
from jax.experimental import pallas as pl
from jax.experimental.pallas import tpu as pltpu
from jax.sharding import PartitionSpec as P

BLOCK = 256
RING = 4
PARTS = 2
F32 = jnp.float32
BF16 = jnp.bfloat16
IN_VMEM = pl.BlockSpec(memory_space=pltpu.VMEM)
IN_HBM = pl.BlockSpec(memory_space=pltpu.HBM)
IN_SMEM = pl.BlockSpec(memory_space=pltpu.SMEM)
VMEM_BYTES = 28 * 1024 * 1024
LOADING_BYTES = 47 * 1024 * 1024
FORWARD, BACKWARD, OPEN_F, OPEN_B, AROUND = 0, 20, 40, 44, 48
TABLE = 52


def along_y(block, flip, groups):
    route = [(z * RING + y, z * RING + (y ^ flip)) for z in range(groups) for y in range(RING)]
    return lax.ppermute(block, "seq", route)


def along_z(block, distance, groups):
    route = [
        (z * RING + y, (z + distance) % groups * RING + y) for z in range(groups) for y in range(RING)
    ]
    return lax.ppermute(block, "seq", route)


def dot(left, right, left_dim, right_dim):
    return lax.dot_general(
        left, right, (((left_dim,), (right_dim,)), ((), ())), preferred_element_type=F32
    )


def ends_of(lens):
    ends, total = [], jnp.int32(0)
    for d in range(lens.shape[0]):
        total = total + lens[d]
        ends.append(total)
    return ends


def start_at(ends, position):
    start = jnp.int32(0)
    for end in ends:
        start = jnp.where(end <= position, end, start)
    return start


def end_at(ends, position):
    found = jnp.int32(1 << 20)
    for end in reversed(ends):
        found = jnp.where(end > position, end, found)
    return found


def rows_where(shape, dim, low, high):
    places = lax.broadcasted_iota(jnp.int32, shape, dim)
    return ((places >= low) & (places < high)).astype(F32)


def addend_kernel(heads, groups, rank, lens, *refs):
    given, outs, major = refs[:4], refs[4 : 4 + RING * PARTS], refs[4 + RING * PARTS : 8 + RING * PARTS]
    table, landed, sems = refs[8 + RING * PARTS], refs[9 + RING * PARTS : 13 + RING * PARTS], refs[13 + RING * PARTS]
    copies = [pltpu.make_async_copy(src, dst, sems.at[i]) for i, (src, dst) in enumerate(zip(given, landed))]
    for copy in copies:
        copy.start()
    rows, width = given[0].shape[0], given[0].shape[2]
    first = rank[0] * rows
    ring = lax.rem(rank[0], RING)
    ends = ends_of(lens)
    fill_table(groups, rank[0], rows, ends, table)
    tail_from = start_at(ends, first + rows) - first
    head_to = jnp.where(first > 0, end_at(ends, first - 1) - first, 0)
    tail = rows_where((rows, width), 0, tail_from, rows).astype(BF16)
    head = rows_where((rows, width), 0, 0, head_to).astype(BF16)
    for copy, src, dst in zip(copies, landed, major):
        copy.wait()
        dst[...] = jnp.swapaxes(src[...], 0, 1)
    ks, vs, qs, cs = major
    own = heads // (RING * PARTS)
    for part in range(PARTS):
        for r in range(RING):
            owner = lax.bitwise_xor(ring, r)
            for j in range(own):
                h = part * (heads // PARTS) + owner * own + j
                outs[part * RING + r][0, j] = dot(ks[h] * tail, vs[h], 0, 0)
                outs[part * RING + r][1, j] = dot(qs[h] * head, cs[h], 0, 0)


def fill_table(groups, rank, rows, ends, table):
    def same(a, b):
        cut = jnp.int32(0)
        for end in ends:
            cut = cut | ((end > a) & (end <= b)).astype(jnp.int32)
        return 1 - cut

    start = lax.div(rank, RING) * RING * rows
    step_f = [same(start + j * rows, start + (j + 1) * rows) for j in range(RING)]
    step_b = [same(start + j * rows - 1, start + (j + 1) * rows - 1) for j in range(RING)]
    for t in range(RING + 1):
        for s in range(RING):
            weight = jnp.int32(1 if s < t else 0)
            for j in range(s + 1, t):
                weight = weight * step_f[j]
            table[FORWARD + t * RING + s] = weight.astype(F32)
    for t in range(RING + 1):
        for s in range(RING):
            weight = jnp.int32(1 if s > t - 1 else 0)
            for j in range(t, s):
                weight = weight * step_b[j]
            table[BACKWARD + t * RING + s] = weight.astype(F32)
    weight = jnp.int32(1)
    for t in range(RING):
        table[OPEN_F + t] = weight.astype(F32)
        weight = weight * step_f[t]
    weight = jnp.int32(1)
    for t in reversed(range(RING)):
        table[OPEN_B + t] = weight.astype(F32)
        weight = weight * step_b[t]
    group = lax.div(rank, RING)
    far_f = same(start - RING * rows, start) * (group > 1).astype(jnp.int32)
    far_b = same(start + RING * rows - 1, start + 2 * RING * rows - 1) * (group < groups - 2).astype(jnp.int32)
    table[AROUND] = (group > 0).astype(F32)
    table[AROUND + 1] = far_f.astype(F32)
    table[AROUND + 2] = (group < groups - 1).astype(F32)
    table[AROUND + 3] = far_b.astype(F32)


def inner_kernel(base, rank, lens, ks, vs, qs, cs, att, gq, gk, gv):
    rows, width = qs.shape[1], qs.shape[2]
    factor = (width * BLOCK) ** (-0.5)
    first = rank[0] * rows
    ends = ends_of(lens)
    t_at = first + lax.broadcasted_iota(jnp.int32, (rows, rows), 0)
    s_at = first + lax.broadcasted_iota(jnp.int32, (rows, rows), 1)
    end_of = jnp.full((1, rows), 1 << 20, jnp.int32)
    lane = first + lax.broadcasted_iota(jnp.int32, (1, rows), 1)
    for end in reversed(ends):
        end_of = jnp.where(lane < end, end, end_of)
    visible = jnp.where((t_at >= s_at) & (t_at < end_of), factor, 0.0)

    def one(h, carry):
        qh, kh, vh, ch = qs[base + h], ks[base + h], vs[base + h], cs[base + h]
        weights = (visible * dot(qh, kh, 1, 1)).astype(BF16)
        grads = (visible * dot(ch, vh, 1, 1)).astype(BF16)
        att[h] = dot(weights, vh, 1, 0).astype(BF16)
        gq[h] = dot(grads, kh, 1, 0).astype(BF16)
        gk[h] = dot(grads, qh, 0, 0).astype(BF16)
        gv[h] = dot(weights, ch, 0, 0).astype(BF16)
        return carry

    lax.fori_loop(0, att.shape[0], one, 0, unroll=2)


def total_kernel(rank, table, *refs):
    held, (total_f, total_b) = refs[:RING], refs[RING:]
    ring = lax.rem(rank[0], RING)
    for direction, out, row in ((0, total_f, FORWARD + RING * RING), (1, total_b, BACKWARD)):
        total = None
        for r in range(RING):
            source = lax.bitwise_xor(ring, r)
            term = table[row + source] * held[r][direction]
            total = term if total is None else total + term
        out[...] = total


def carry_kernel(rank, table, *refs):
    held, (near_f, far_f, near_b, far_b), outs = refs[:RING], refs[RING : RING + 4], refs[RING + 4 :]
    ring = lax.rem(rank[0], RING)
    into = (
        table[AROUND] * near_f[...] + table[AROUND + 1] * far_f[...],
        table[AROUND + 2] * near_b[...] + table[AROUND + 3] * far_b[...],
    )
    for r in range(RING):
        target = lax.bitwise_xor(ring, r)
        for direction in range(2):
            row = FORWARD + target * RING if direction == 0 else BACKWARD + (target + 1) * RING
            total = table[(OPEN_F if direction == 0 else OPEN_B) + target] * into[direction]
            for s in range(RING):
                source = lax.bitwise_xor(ring, s)
                total = total + table[row + source] * held[s][direction]
            outs[r][direction] = total


def outer_kernel(part, heads, rank, lens, ks, vs, qs, cs, *refs):
    inner, states, rest = refs[:4], refs[4 : 4 + RING], refs[4 + RING :]
    rows, width = qs.shape[1], qs.shape[2]
    factor = (width * BLOCK) ** (-0.5)
    first = rank[0] * rows
    ring = lax.rem(rank[0], RING)
    ends = ends_of(lens)
    head = factor * rows_where((rows, width), 0, 0, end_at(ends, first) - first)
    tail = factor * rows_where((rows, width), 0, start_at(ends, first + rows - 1) - first, rows)
    own = heads // (RING * PARTS)
    base = part * (heads // PARTS)
    last = part == PARTS - 1
    if last:
        earlier, outs = rest[: 4 * (PARTS - 1)], rest[4 * (PARTS - 1) : 4 * PARTS]
        joined, ready, sems = rest[4 * PARTS], rest[4 * PARTS + 1], rest[4 * PARTS + 2]
    copies = []
    for i, (left, side, scale, dim) in enumerate(((qs, 0, head, 0), (cs, 0, head, 1), (vs, 1, tail, 1), (ks, 1, tail, 0))):
        result = joined if last else rest[i]
        if last:
            for p in range(PARTS - 1):
                joined[p * (heads // PARTS) : (p + 1) * (heads // PARTS)] = earlier[4 * p + i][...]
        for r in range(RING):
            owner = lax.bitwise_xor(ring, r)
            for j in range(own):
                h = owner * own + j
                term = dot(left[base + h], states[r][side, j].astype(BF16), 1, dim)
                at = base + h if last else h
                result[at] = (inner[i][h].astype(F32) + scale * term).astype(BF16)
        if last:
            ready[i] = jnp.swapaxes(joined[...], 0, 1)
            copies.append(pltpu.make_async_copy(ready.at[i], outs[i], sems.at[i]))
            copies[-1].start()
    for copy in copies:
        copy.wait()


def local(queries, keys, values, cotangent, doc_lengths):
    rows, heads, width = queries.shape
    groups = lax.axis_size("seq") // RING
    rank = lax.axis_index("seq").astype(jnp.int32).reshape(1)
    own = heads // (RING * PARTS)
    shape = jax.ShapeDtypeStruct
    chunk = shape((2, own, width, width), F32)
    single = shape((own, width, width), F32)
    major = shape((heads, rows, width), BF16)

    def call(kernel, name, scalars, operands, in_specs, out_shape, out_specs=None, scratch=(), aliases=None, flops=0, vmem=VMEM_BYTES):
        return pl.pallas_call(
            kernel,
            out_shape=out_shape,
            in_specs=[IN_SMEM] * len(scalars) + in_specs,
            out_specs=out_specs or [IN_VMEM] * len(out_shape),
            scratch_shapes=list(scratch),
            input_output_aliases=aliases or {},
            compiler_params=pltpu.CompilerParams(vmem_limit_bytes=vmem),
            cost_estimate=pl.CostEstimate(flops=flops, bytes_accessed=1 << 20, transcendentals=0),
            name=name,
        )(*scalars, *operands)

    place = (rank, doc_lengths)
    made = call(
        functools.partial(addend_kernel, heads, groups), "addends", place, (keys, values, queries, cotangent), [IN_HBM] * 4,
        [chunk] * (RING * PARTS) + [major] * 4 + [shape((TABLE,), F32)],
        [IN_VMEM] * (RING * PARTS + 4) + [IN_SMEM],
        scratch=[pltpu.VMEM((rows, heads, width), BF16)] * 4 + [pltpu.SemaphoreType.DMA((4,))], flops=4 * 10**9, vmem=LOADING_BYTES,
    )
    in_major, table = made[RING * PARTS : RING * PARTS + 4], made[-1]
    held = []
    for part in range(PARTS):
        mine = list(made[part * RING : (part + 1) * RING])
        if part:
            held[-1][1], mine = lax.optimization_barrier((held[-1][1], mine))
        held.append([along_y(mine[r], r, groups) if r else mine[0] for r in range(RING)])
    some = shape((heads // PARTS, rows, width), BF16)

    def inner_of(part, operands):
        return call(
            functools.partial(inner_kernel, part * (heads // PARTS)), f"inner{part}", place, operands, [IN_VMEM] * 4,
            [some] * 4, flops=4 * 10**9,
        )

    inner = [inner_of(0, in_major), None]
    states = []
    held[0], inner[0] = lax.optimization_barrier((held[0], inner[0]))
    for part in range(PARTS):
        total_f, total_b = call(
            total_kernel, f"totals{part}", (rank, table), held[part], [IN_VMEM] * RING, [single] * 2
        )
        near_f, near_b = along_z(total_f, 1, groups), along_z(total_b, -1, groups)
        far_f, far_b = along_z(near_f, 1, groups), along_z(near_b, -1, groups)
        carries = call(
            carry_kernel, f"carries{part}", (rank, table), held[part] + [near_f, far_f, near_b, far_b],
            [IN_VMEM] * (RING + 4), [chunk] * RING,
        )
        if part:
            states[-1][1], carries, late = lax.optimization_barrier((states[-1][1], carries, in_major))
            inner[part] = inner_of(part, late)
        states.append([along_y(carries[r], r, groups) if r else carries[0] for r in range(RING)])
    earlier = []
    for part in range(PARTS - 1):
        earlier += call(
            functools.partial(outer_kernel, part, heads), f"outer{part}", place,
            (*in_major, *inner[part], *states[part]), [IN_VMEM] * (8 + RING), [some] * 4,
        )
    whole = shape((rows, heads, width), BF16)
    return tuple(
        call(
            functools.partial(outer_kernel, PARTS - 1, heads), f"outer{PARTS - 1}", place,
            (*in_major, *inner[-1], *states[-1], *earlier), [IN_VMEM] * (8 + RING + 4 * (PARTS - 1)),
            [whole] * 4, [IN_HBM] * 4,
            scratch=[
                pltpu.VMEM((heads, rows, width), BF16),
                pltpu.VMEM((4, rows, heads, width), BF16),
                pltpu.SemaphoreType.DMA((4,)),
            ],
        )
    )


def solution(mesh):
    rows = P(("dp", "seq"), None, None)
    return jax.shard_map(
        local, mesh=mesh, in_specs=(rows, rows, rows, rows, P("dp")), out_specs=(rows,) * 4, check_vma=False
    )
```

```python
import functools

import jax
import jax.numpy as jnp
from jax import lax
from jax.experimental import pallas as pl
from jax.experimental.pallas import tpu as pltpu
from jax.sharding import PartitionSpec as P

BLOCK = 256
RING = 4
PARTS = 2
HALVES = 2
F32 = jnp.float32
BF16 = jnp.bfloat16
IN_VMEM = pl.BlockSpec(memory_space=pltpu.VMEM)
IN_HBM = pl.BlockSpec(memory_space=pltpu.HBM)
IN_SMEM = pl.BlockSpec(memory_space=pltpu.SMEM)
VMEM_BYTES = 28 * 1024 * 1024
LOADING_BYTES = 48 * 1024 * 1024
FORWARD, BACKWARD, OPEN_F, OPEN_B, AROUND = 0, 20, 40, 44, 48
TABLE = 52


def along_y(block, flip, groups):
    route = [(z * RING + y, z * RING + (y ^ flip)) for z in range(groups) for y in range(RING)]
    return lax.ppermute(block, "seq", route)


def along_z(block, distance, groups):
    route = [
        (z * RING + y, (z + distance) % groups * RING + y) for z in range(groups) for y in range(RING)
    ]
    return lax.ppermute(block, "seq", route)


def dot(left, right, left_dim, right_dim):
    return lax.dot_general(
        left, right, (((left_dim,), (right_dim,)), ((), ())), preferred_element_type=F32
    )


def ends_of(lens):
    ends, total = [], jnp.int32(0)
    for d in range(lens.shape[0]):
        total = total + lens[d]
        ends.append(total)
    return ends


def start_at(ends, position):
    start = jnp.int32(0)
    for end in ends:
        start = jnp.where(end <= position, end, start)
    return start


def end_at(ends, position):
    found = jnp.int32(1 << 20)
    for end in reversed(ends):
        found = jnp.where(end > position, end, found)
    return found


def rows_where(shape, dim, low, high):
    places = lax.broadcasted_iota(jnp.int32, shape, dim)
    return ((places >= low) & (places < high)).astype(F32)


def addend_kernel(part, heads, groups, rank, lens, *refs):
    if part == 0:
        given, outs, major, table, landed, sems = refs[:4], refs[4:8], refs[8:12], refs[12], refs[13:17], refs[17]
        copies = [pltpu.make_async_copy(src, dst, sems.at[i]) for i, (src, dst) in enumerate(zip(given, landed))]
        for copy in copies:
            copy.start()
    else:
        major, outs = refs[:4], refs[4:8]
    rows, width = BLOCK, outs[0].shape[-1]
    first = rank[0] * rows
    ring = lax.rem(rank[0], RING)
    ends = ends_of(lens)
    tail_from = start_at(ends, first + rows) - first
    head_to = jnp.where(first > 0, end_at(ends, first - 1) - first, 0)
    tail = rows_where((rows, width), 0, tail_from, rows).astype(BF16)
    head = rows_where((rows, width), 0, 0, head_to).astype(BF16)
    if part == 0:
        fill_table(groups, rank[0], rows, ends, table)
        for copy, src, dst in zip(copies, landed, major):
            copy.wait()
            dst[...] = jnp.swapaxes(src[...], 0, 1)
    ks, vs, qs, cs = major
    own = heads // (RING * PARTS)
    for r in range(RING):
        owner = lax.bitwise_xor(ring, r)
        for j in range(own):
            h = part * (heads // PARTS) + owner * own + j
            outs[r][0, j] = dot(ks[h] * tail, vs[h], 0, 0)
            outs[r][1, j] = dot(qs[h] * head, cs[h], 0, 0)


def fill_table(groups, rank, rows, ends, table):
    def same(a, b):
        cut = jnp.int32(0)
        for end in ends:
            cut = cut | ((end > a) & (end <= b)).astype(jnp.int32)
        return 1 - cut

    start = lax.div(rank, RING) * RING * rows
    step_f = [same(start + j * rows, start + (j + 1) * rows) for j in range(RING)]
    step_b = [same(start + j * rows - 1, start + (j + 1) * rows - 1) for j in range(RING)]
    for t in range(RING + 1):
        for s in range(RING):
            weight = jnp.int32(1 if s < t else 0)
            for j in range(s + 1, t):
                weight = weight * step_f[j]
            table[FORWARD + t * RING + s] = weight.astype(F32)
    for t in range(RING + 1):
        for s in range(RING):
            weight = jnp.int32(1 if s > t - 1 else 0)
            for j in range(t, s):
                weight = weight * step_b[j]
            table[BACKWARD + t * RING + s] = weight.astype(F32)
    weight = jnp.int32(1)
    for t in range(RING):
        table[OPEN_F + t] = weight.astype(F32)
        weight = weight * step_f[t]
    weight = jnp.int32(1)
    for t in reversed(range(RING)):
        table[OPEN_B + t] = weight.astype(F32)
        weight = weight * step_b[t]
    group = lax.div(rank, RING)
    far_f = same(start - RING * rows, start) * (group > 1).astype(jnp.int32)
    far_b = same(start + RING * rows - 1, start + 2 * RING * rows - 1) * (group < groups - 2).astype(jnp.int32)
    table[AROUND] = (group > 0).astype(F32)
    table[AROUND + 1] = far_f.astype(F32)
    table[AROUND + 2] = (group < groups - 1).astype(F32)
    table[AROUND + 3] = far_b.astype(F32)


def inner_kernel(base, rank, lens, ks, vs, qs, cs, att, gq, gk, gv):
    rows, width = qs.shape[1], qs.shape[2]
    factor = (width * BLOCK) ** (-0.5)
    first = rank[0] * rows
    ends = ends_of(lens)
    t_at = first + lax.broadcasted_iota(jnp.int32, (rows, rows), 0)
    s_at = first + lax.broadcasted_iota(jnp.int32, (rows, rows), 1)
    end_of = jnp.full((1, rows), 1 << 20, jnp.int32)
    lane = first + lax.broadcasted_iota(jnp.int32, (1, rows), 1)
    for end in reversed(ends):
        end_of = jnp.where(lane < end, end, end_of)
    visible = jnp.where((t_at >= s_at) & (t_at < end_of), factor, 0.0)

    def one(h, carry):
        qh, kh, vh, ch = qs[base + h], ks[base + h], vs[base + h], cs[base + h]
        weights = (visible * dot(qh, kh, 1, 1)).astype(BF16)
        grads = (visible * dot(ch, vh, 1, 1)).astype(BF16)
        att[h] = dot(weights, vh, 1, 0).astype(BF16)
        gq[h] = dot(grads, kh, 1, 0).astype(BF16)
        gk[h] = dot(grads, qh, 0, 0).astype(BF16)
        gv[h] = dot(weights, ch, 0, 0).astype(BF16)
        return carry

    lax.fori_loop(0, att.shape[0], one, 0, unroll=2)


def total_kernel(rank, table, *refs):
    held, (total_f, total_b) = refs[:RING], refs[RING:]
    ring = lax.rem(rank[0], RING)
    for direction, out, row in ((0, total_f, FORWARD + RING * RING), (1, total_b, BACKWARD)):
        total = None
        for r in range(RING):
            source = lax.bitwise_xor(ring, r)
            term = table[row + source] * held[r][direction]
            total = term if total is None else total + term
        out[...] = total


def carry_kernel(rank, table, *refs):
    held, (near_f, far_f, near_b, far_b), outs = refs[:RING], refs[RING : RING + 4], refs[RING + 4 :]
    ring = lax.rem(rank[0], RING)
    into = (
        table[AROUND] * near_f[...] + table[AROUND + 1] * far_f[...],
        table[AROUND + 2] * near_b[...] + table[AROUND + 3] * far_b[...],
    )
    for r in range(RING):
        target = lax.bitwise_xor(ring, r)
        for direction in range(2):
            row = FORWARD + target * RING if direction == 0 else BACKWARD + (target + 1) * RING
            total = table[(OPEN_F if direction == 0 else OPEN_B) + target] * into[direction]
            for s in range(RING):
                source = lax.bitwise_xor(ring, s)
                total = total + table[row + source] * held[s][direction]
            outs[r][direction] = total


def outer_kernel(part, heads, rank, lens, ks, vs, qs, cs, *refs):
    inner, states, rest = refs[:4], refs[4 : 4 + RING], refs[4 + RING :]
    rows, width = qs.shape[1], qs.shape[2]
    factor = (width * BLOCK) ** (-0.5)
    first = rank[0] * rows
    ring = lax.rem(rank[0], RING)
    ends = ends_of(lens)
    head = factor * rows_where((rows, width), 0, 0, end_at(ends, first) - first)
    tail = factor * rows_where((rows, width), 0, start_at(ends, first + rows - 1) - first, rows)
    own = heads // (RING * PARTS)
    base = part * (heads // PARTS)
    last = part == PARTS - 1
    if last:
        earlier, outs = rest[: 4 * (PARTS - 1)], rest[4 * (PARTS - 1) : 4 * PARTS]
        joined, ready, sems = rest[4 * PARTS], rest[4 * PARTS + 1], rest[4 * PARTS + 2]
    copies = []
    for i, (left, side, scale, dim) in enumerate(((qs, 0, head, 0), (cs, 0, head, 1), (vs, 1, tail, 1), (ks, 1, tail, 0))):
        result = joined if last else rest[i]
        if last:
            for p in range(PARTS - 1):
                joined[p * (heads // PARTS) : (p + 1) * (heads // PARTS)] = earlier[4 * p + i][...]
        for r in range(RING):
            owner = lax.bitwise_xor(ring, r)
            for j in range(own):
                h = owner * own + j
                term = dot(left[base + h], states[r][side, j].astype(BF16), 1, dim)
                at = base + h if last else h
                result[at] = (inner[i][h].astype(F32) + scale * term).astype(BF16)
        if last:
            for half in range(HALVES):
                some = pl.ds(half * (rows // HALVES), rows // HALVES)
                ready[i, some] = jnp.swapaxes(joined[:, some, :], 0, 1)
                copies.append(pltpu.make_async_copy(ready.at[i, some], outs[i].at[some], sems.at[i, half]))
                copies[-1].start()
    for copy in copies:
        copy.wait()


def local(queries, keys, values, cotangent, doc_lengths):
    rows, heads, width = queries.shape
    groups = lax.axis_size("seq") // RING
    rank = lax.axis_index("seq").astype(jnp.int32).reshape(1)
    own = heads // (RING * PARTS)
    shape = jax.ShapeDtypeStruct
    chunk = shape((2, own, width, width), F32)
    single = shape((own, width, width), F32)
    major = shape((heads, rows, width), BF16)

    def call(kernel, name, scalars, operands, in_specs, out_shape, out_specs=None, scratch=(), aliases=None, flops=0, vmem=VMEM_BYTES):
        return pl.pallas_call(
            kernel,
            out_shape=out_shape,
            in_specs=[IN_SMEM] * len(scalars) + in_specs,
            out_specs=out_specs or [IN_VMEM] * len(out_shape),
            scratch_shapes=list(scratch),
            input_output_aliases=aliases or {},
            compiler_params=pltpu.CompilerParams(vmem_limit_bytes=vmem),
            cost_estimate=pl.CostEstimate(flops=flops, bytes_accessed=1 << 20, transcendentals=0),
            name=name,
        )(*scalars, *operands)

    place = (rank, doc_lengths)
    *mine, ks, vs, qs, cs, table = call(
        functools.partial(addend_kernel, 0, heads, groups), "addends0", place, (keys, values, queries, cotangent),
        [IN_HBM] * 4, [chunk] * RING + [major] * 4 + [shape((TABLE,), F32)], [IN_VMEM] * (RING + 4) + [IN_SMEM],
        scratch=[pltpu.VMEM((rows, heads, width), BF16)] * 4 + [pltpu.SemaphoreType.DMA((4,))],
        flops=4 * 10**9, vmem=LOADING_BYTES,
    )
    in_major = (ks, vs, qs, cs)
    held = []
    for part in range(PARTS):
        if part:
            mine = call(
                functools.partial(addend_kernel, part, heads, groups), f"addends{part}", place, in_major,
                [IN_VMEM] * 4, [chunk] * RING, flops=10**9,
            )
        held.append([along_y(mine[r], r, groups) if r else mine[0] for r in range(RING)])
    some = shape((heads // PARTS, rows, width), BF16)

    def inner_of(part, operands):
        return call(
            functools.partial(inner_kernel, part * (heads // PARTS)), f"inner{part}", place, operands, [IN_VMEM] * 4,
            [some] * 4, flops=4 * 10**9,
        )

    inner = [inner_of(0, in_major), None]
    states = []
    held[0], inner[0] = lax.optimization_barrier((held[0], inner[0]))
    for part in range(PARTS):
        total_f, total_b = call(
            total_kernel, f"totals{part}", (rank, table), held[part], [IN_VMEM] * RING, [single] * 2
        )
        near_f, near_b = along_z(total_f, 1, groups), along_z(total_b, -1, groups)
        far_f, far_b = along_z(near_f, 1, groups), along_z(near_b, -1, groups)
        carries = call(
            carry_kernel, f"carries{part}", (rank, table), held[part] + [near_f, far_f, near_b, far_b],
            [IN_VMEM] * (RING + 4), [chunk] * RING,
        )
        if part:
            states[-1][1], carries, late = lax.optimization_barrier((states[-1][1], carries, in_major))
            inner[part] = inner_of(part, late)
        states.append([along_y(carries[r], r, groups) if r else carries[0] for r in range(RING)])
    earlier = []
    for part in range(PARTS - 1):
        earlier += call(
            functools.partial(outer_kernel, part, heads), f"outer{part}", place,
            (*in_major, *inner[part], *states[part]), [IN_VMEM] * (8 + RING), [some] * 4,
        )
    whole = shape((rows, heads, width), BF16)
    return tuple(
        call(
            functools.partial(outer_kernel, PARTS - 1, heads), f"outer{PARTS - 1}", place,
            (*in_major, *inner[-1], *states[-1], *earlier), [IN_VMEM] * (8 + RING + 4 * (PARTS - 1)),
            [whole] * 4, [IN_HBM] * 4,
            scratch=[
                pltpu.VMEM((heads, rows, width), BF16),
                pltpu.VMEM((4, rows, heads, width), BF16),
                pltpu.SemaphoreType.DMA((4, HALVES)),
            ],
        )
    )


def solution(mesh):
    rows = P(("dp", "seq"), None, None)
    return jax.shard_map(
        local, mesh=mesh, in_specs=(rows, rows, rows, rows, P("dp")), out_specs=(rows,) * 4, check_vma=False
    )
```

```python
import functools

import jax
import jax.numpy as jnp
from jax import lax
from jax.experimental import pallas as pl
from jax.experimental.pallas import tpu as pltpu
from jax.sharding import PartitionSpec as P

BLOCK = 256
RING = 4
FLIPS = (0, 1, 3, 2)
FIRST = 1
PARTS = 2
HALVES = 2
F32 = jnp.float32
BF16 = jnp.bfloat16
IN_VMEM = pl.BlockSpec(memory_space=pltpu.VMEM)
IN_HBM = pl.BlockSpec(memory_space=pltpu.HBM)
IN_SMEM = pl.BlockSpec(memory_space=pltpu.SMEM)
VMEM_BYTES = 28 * 1024 * 1024
LOADING_BYTES = 48 * 1024 * 1024
FORWARD, BACKWARD, OPEN_F, OPEN_B, AROUND = 0, 20, 40, 44, 48
TABLE = 52


def along_y(block, flip, groups):
    route = [(z * RING + y, z * RING + (y ^ flip)) for z in range(groups) for y in range(RING)]
    return lax.ppermute(block, "seq", route)


def along_z(block, distance, groups):
    route = [
        (z * RING + y, (z + distance) % groups * RING + y) for z in range(groups) for y in range(RING)
    ]
    return lax.ppermute(block, "seq", route)


def dot(left, right, left_dim, right_dim):
    return lax.dot_general(
        left, right, (((left_dim,), (right_dim,)), ((), ())), preferred_element_type=F32
    )


def ends_of(lens):
    ends, total = [], jnp.int32(0)
    for d in range(lens.shape[0]):
        total = total + lens[d]
        ends.append(total)
    return ends


def start_at(ends, position):
    start = jnp.int32(0)
    for end in ends:
        start = jnp.where(end <= position, end, start)
    return start


def end_at(ends, position):
    found = jnp.int32(1 << 20)
    for end in reversed(ends):
        found = jnp.where(end > position, end, found)
    return found


def rows_where(shape, dim, low, high):
    places = lax.broadcasted_iota(jnp.int32, shape, dim)
    return ((places >= low) & (places < high)).astype(F32)


def addend_kernel(part, heads, groups, rank, lens, *refs):
    if part == 0:
        given, outs, major, table, landed, sems = refs[:4], refs[4:8], refs[8:12], refs[12], refs[13:17], refs[17]
        copies = [pltpu.make_async_copy(src, dst, sems.at[i]) for i, (src, dst) in enumerate(zip(given, landed))]
        for copy in copies:
            copy.start()
    else:
        major, outs = refs[:4], refs[4:8]
    rows, width = BLOCK, outs[0].shape[-1]
    first = rank[0] * rows
    ring = lax.rem(rank[0], RING)
    ends = ends_of(lens)
    tail_from = start_at(ends, first + rows) - first
    head_to = jnp.where(first > 0, end_at(ends, first - 1) - first, 0)
    tail = rows_where((rows, width), 0, tail_from, rows).astype(BF16)
    head = rows_where((rows, width), 0, 0, head_to).astype(BF16)
    if part == 0:
        fill_table(groups, rank[0], rows, ends, table)
        for copy, src, dst in zip(copies, landed, major):
            copy.wait()
            dst[...] = jnp.swapaxes(src[...], 0, 1)
    ks, vs, qs, cs = major
    own = heads // (RING * PARTS)
    for r in range(RING):
        owner = lax.bitwise_xor(ring, FLIPS[r])
        for j in range(own):
            h = part * (heads // PARTS) + owner * own + j
            outs[r][0, j] = dot(ks[h] * tail, vs[h], 0, 0)
            outs[r][1, j] = dot(qs[h] * head, cs[h], 0, 0)


def fill_table(groups, rank, rows, ends, table):
    def same(a, b):
        cut = jnp.int32(0)
        for end in ends:
            cut = cut | ((end > a) & (end <= b)).astype(jnp.int32)
        return 1 - cut

    start = lax.div(rank, RING) * RING * rows
    step_f = [same(start + j * rows, start + (j + 1) * rows) for j in range(RING)]
    step_b = [same(start + j * rows - 1, start + (j + 1) * rows - 1) for j in range(RING)]
    for t in range(RING + 1):
        for s in range(RING):
            weight = jnp.int32(1 if s < t else 0)
            for j in range(s + 1, t):
                weight = weight * step_f[j]
            table[FORWARD + t * RING + s] = weight.astype(F32)
    for t in range(RING + 1):
        for s in range(RING):
            weight = jnp.int32(1 if s > t - 1 else 0)
            for j in range(t, s):
                weight = weight * step_b[j]
            table[BACKWARD + t * RING + s] = weight.astype(F32)
    weight = jnp.int32(1)
    for t in range(RING):
        table[OPEN_F + t] = weight.astype(F32)
        weight = weight * step_f[t]
    weight = jnp.int32(1)
    for t in reversed(range(RING)):
        table[OPEN_B + t] = weight.astype(F32)
        weight = weight * step_b[t]
    group = lax.div(rank, RING)
    far_f = same(start - RING * rows, start) * (group > 1).astype(jnp.int32)
    far_b = same(start + RING * rows - 1, start + 2 * RING * rows - 1) * (group < groups - 2).astype(jnp.int32)
    table[AROUND] = (group > 0).astype(F32)
    table[AROUND + 1] = far_f.astype(F32)
    table[AROUND + 2] = (group < groups - 1).astype(F32)
    table[AROUND + 3] = far_b.astype(F32)


def inner_kernel(base, rank, lens, ks, vs, qs, cs, att, gq, gk, gv):
    rows, width = qs.shape[1], qs.shape[2]
    factor = (width * BLOCK) ** (-0.5)
    first = rank[0] * rows
    ends = ends_of(lens)
    t_at = first + lax.broadcasted_iota(jnp.int32, (rows, rows), 0)
    s_at = first + lax.broadcasted_iota(jnp.int32, (rows, rows), 1)
    end_of = jnp.full((1, rows), 1 << 20, jnp.int32)
    lane = first + lax.broadcasted_iota(jnp.int32, (1, rows), 1)
    for end in reversed(ends):
        end_of = jnp.where(lane < end, end, end_of)
    visible = jnp.where((t_at >= s_at) & (t_at < end_of), factor, 0.0)

    def one(h, carry):
        qh, kh, vh, ch = qs[base + h], ks[base + h], vs[base + h], cs[base + h]
        weights = (visible * dot(qh, kh, 1, 1)).astype(BF16)
        grads = (visible * dot(ch, vh, 1, 1)).astype(BF16)
        att[h] = dot(weights, vh, 1, 0).astype(BF16)
        gq[h] = dot(grads, kh, 1, 0).astype(BF16)
        gk[h] = dot(grads, qh, 0, 0).astype(BF16)
        gv[h] = dot(weights, ch, 0, 0).astype(BF16)
        return carry

    lax.fori_loop(0, att.shape[0], one, 0, unroll=2)


def total_kernel(rank, table, *refs):
    held, (total_f, total_b) = refs[:RING], refs[RING:]
    ring = lax.rem(rank[0], RING)
    for direction, out, row in ((0, total_f, FORWARD + RING * RING), (1, total_b, BACKWARD)):
        total = None
        for r in range(RING):
            source = lax.bitwise_xor(ring, FLIPS[r])
            term = table[row + source] * held[r][direction]
            total = term if total is None else total + term
        out[...] = total


def carry_kernel(rank, table, *refs):
    held, (near_f, far_f, near_b, far_b), outs = refs[:RING], refs[RING : RING + 4], refs[RING + 4 :]
    ring = lax.rem(rank[0], RING)
    into = (
        table[AROUND] * near_f[...] + table[AROUND + 1] * far_f[...],
        table[AROUND + 2] * near_b[...] + table[AROUND + 3] * far_b[...],
    )
    for r in range(RING):
        target = lax.bitwise_xor(ring, FLIPS[r])
        for direction in range(2):
            row = FORWARD + target * RING if direction == 0 else BACKWARD + (target + 1) * RING
            total = table[(OPEN_F if direction == 0 else OPEN_B) + target] * into[direction]
            for s in range(RING):
                source = lax.bitwise_xor(ring, FLIPS[s])
                total = total + table[row + source] * held[s][direction]
            outs[r][direction] = total


def outer_kernel(part, heads, rank, lens, ks, vs, qs, cs, *refs):
    inner, states, rest = refs[:4], refs[4 : 4 + RING], refs[4 + RING :]
    rows, width = qs.shape[1], qs.shape[2]
    factor = (width * BLOCK) ** (-0.5)
    first = rank[0] * rows
    ring = lax.rem(rank[0], RING)
    ends = ends_of(lens)
    head = factor * rows_where((rows, width), 0, 0, end_at(ends, first) - first)
    tail = factor * rows_where((rows, width), 0, start_at(ends, first + rows - 1) - first, rows)
    own = heads // (RING * PARTS)
    base = part * (heads // PARTS)
    last = part == PARTS - 1
    if last:
        earlier, outs = rest[: 4 * (PARTS - 1)], rest[4 * (PARTS - 1) : 4 * PARTS]
        joined, ready, sems = rest[4 * PARTS], rest[4 * PARTS + 1], rest[4 * PARTS + 2]
    copies = []
    for i, (left, side, scale, dim) in enumerate(((qs, 0, head, 0), (cs, 0, head, 1), (vs, 1, tail, 1), (ks, 1, tail, 0))):
        result = joined if last else rest[i]
        if last:
            for p in range(PARTS - 1):
                joined[p * (heads // PARTS) : (p + 1) * (heads // PARTS)] = earlier[4 * p + i][...]
        for r in range(RING):
            owner = lax.bitwise_xor(ring, FLIPS[r])
            for j in range(own):
                h = owner * own + j
                term = dot(left[base + h], states[r][side, j].astype(BF16), 1, dim)
                at = base + h if last else h
                result[at] = (inner[i][h].astype(F32) + scale * term).astype(BF16)
        if last:
            for half in range(HALVES):
                some = pl.ds(half * (rows // HALVES), rows // HALVES)
                ready[i, some] = jnp.swapaxes(joined[:, some, :], 0, 1)
                copies.append(pltpu.make_async_copy(ready.at[i, some], outs[i].at[some], sems.at[i, half]))
                copies[-1].start()
    for copy in copies:
        copy.wait()


def local(queries, keys, values, cotangent, doc_lengths):
    rows, heads, width = queries.shape
    groups = lax.axis_size("seq") // RING
    rank = lax.axis_index("seq").astype(jnp.int32).reshape(1)
    own = heads // (RING * PARTS)
    shape = jax.ShapeDtypeStruct
    chunk = shape((2, own, width, width), F32)
    single = shape((own, width, width), F32)
    major = shape((heads, rows, width), BF16)

    def call(kernel, name, scalars, operands, in_specs, out_shape, out_specs=None, scratch=(), aliases=None, flops=0, vmem=VMEM_BYTES):
        return pl.pallas_call(
            kernel,
            out_shape=out_shape,
            in_specs=[IN_SMEM] * len(scalars) + in_specs,
            out_specs=out_specs or [IN_VMEM] * len(out_shape),
            scratch_shapes=list(scratch),
            input_output_aliases=aliases or {},
            compiler_params=pltpu.CompilerParams(vmem_limit_bytes=vmem),
            cost_estimate=pl.CostEstimate(flops=flops, bytes_accessed=1 << 20, transcendentals=0),
            name=name,
        )(*scalars, *operands)

    place = (rank, doc_lengths)
    *mine, ks, vs, qs, cs, table = call(
        functools.partial(addend_kernel, 0, heads, groups), "addends0", place, (keys, values, queries, cotangent),
        [IN_HBM] * 4, [chunk] * RING + [major] * 4 + [shape((TABLE,), F32)], [IN_VMEM] * (RING + 4) + [IN_SMEM],
        scratch=[pltpu.VMEM((rows, heads, width), BF16)] * 4 + [pltpu.SemaphoreType.DMA((4,))],
        flops=4 * 10**9, vmem=LOADING_BYTES,
    )
    in_major = (ks, vs, qs, cs)
    held = []
    for part in range(PARTS):
        if part:
            mine = call(
                functools.partial(addend_kernel, part, heads, groups), f"addends{part}", place, in_major,
                [IN_VMEM] * 4, [chunk] * RING, flops=10**9,
            )
        held.append([along_y(mine[r], FLIPS[r], groups) if r else mine[0] for r in range(RING)])
    some = shape((heads // PARTS, rows, width), BF16)

    def inner_of(part, operands):
        return call(
            functools.partial(inner_kernel, part * (heads // PARTS)), f"inner{part}", place, operands, [IN_VMEM] * 4,
            [some] * 4, flops=4 * 10**9,
        )

    inner = [inner_of(0, in_major), None]
    states = []
    held[0], inner[0] = lax.optimization_barrier((held[0], inner[0]))
    for part in range(PARTS):
        total_f, total_b = call(
            total_kernel, f"totals{part}", (rank, table), held[part], [IN_VMEM] * RING, [single] * 2
        )
        near_f, near_b = along_z(total_f, 1, groups), along_z(total_b, -1, groups)
        far_f, far_b = along_z(near_f, 1, groups), along_z(near_b, -1, groups)
        carries = call(
            carry_kernel, f"carries{part}", (rank, table), held[part] + [near_f, far_f, near_b, far_b],
            [IN_VMEM] * (RING + 4), [chunk] * RING,
        )
        if part:
            states[-1][FIRST], carries, late = lax.optimization_barrier((states[-1][FIRST], carries, in_major))
            inner[part] = inner_of(part, late)
        states.append([along_y(carries[r], FLIPS[r], groups) if r else carries[0] for r in range(RING)])
    earlier = []
    for part in range(PARTS - 1):
        earlier += call(
            functools.partial(outer_kernel, part, heads), f"outer{part}", place,
            (*in_major, *inner[part], *states[part]), [IN_VMEM] * (8 + RING), [some] * 4,
        )
    whole = shape((rows, heads, width), BF16)
    return tuple(
        call(
            functools.partial(outer_kernel, PARTS - 1, heads), f"outer{PARTS - 1}", place,
            (*in_major, *inner[-1], *states[-1], *earlier), [IN_VMEM] * (8 + RING + 4 * (PARTS - 1)),
            [whole] * 4, [IN_HBM] * 4,
            scratch=[
                pltpu.VMEM((heads, rows, width), BF16),
                pltpu.VMEM((4, rows, heads, width), BF16),
                pltpu.SemaphoreType.DMA((4, HALVES)),
            ],
        )
    )


def solution(mesh):
    rows = P(("dp", "seq"), None, None)
    return jax.shard_map(
        local, mesh=mesh, in_specs=(rows, rows, rows, rows, P("dp")), out_specs=(rows,) * 4, check_vma=False
    )
```
